32 devices in a mesh: blk: 4 (over x, core), grp: 8 (over z, y).
Axes of the slice: x: 2, y: 2, z: 4, core: 2. Of those that a mesh axis runs over, the one named last changes fastest.
Arguments:
- amplitudes: bfloat16 [8192, 512], P('grp', 'blk'), may hold values from -6 to 6
- amp_tiles: int32 [64, 4], P('grp', 'blk'), may hold values from 0 to 1
- cd_width: int32 [4], P('blk'), may hold values from 64 to 128
- integrals: bfloat16 [8, 128, 4096], P('grp', None, 'blk'), may hold values from -0.25 to 0.25
- int_tiles: int32 [8, 32], P('grp', 'blk'), may hold values 0 or 1
- ab_width: int32 [32], P('blk'), may hold values from 64 to 128
- owners: int32 [4], replicated, may hold values from 0 to 7, as said below
Outputs:
- ladder: bfloat16 [8192, 4096], P('grp', 'blk')
The draws below stay inside these ranges and needn't reach their ends.
Inputs may be any that keep to these rules, and one draw needn't show every extreme that they name: `owners`: the 4 entries are distinct owner slots.
All inputs are finite; a program needn't handle non-finite values. No bound on the sum of `int_tiles` on one device may be relied on, other than what follows from the above.
Results may differ from the reference program's by a relative error of at most 0.001.
Values may be sent and summed in bfloat16 or wider, within the bound.
A program may use at most 64 MiB of HBM per device.

```python
import jax
import jax.numpy as jnp

TILE = 128
ROWS_DEV = 1024
AT = 8
ROWS = 8192
CD = 512
AB = 4096
N_BLK = 4
N_GRP = 8


def draw_amp_tiles(key, part):
    key = jax.random.fold_in(key, 11)
    per_device = ROWS_DEV // TILE
    levels = jax.random.randint(jax.random.fold_in(key, 1), (N_GRP, 1, 1), 1, 5)
    levels = jnp.broadcast_to(levels, (N_GRP, per_device, N_BLK)).reshape(N_GRP * per_device, N_BLK)
    picks = jax.random.randint(jax.random.fold_in(key, 2), (N_GRP * per_device, N_BLK), 0, 4)
    return (picks < levels).astype(jnp.int32)


def draw_owners(key, part):
    key = jax.random.fold_in(key, 23)
    return jax.random.permutation(key, N_GRP)[:N_BLK].astype(jnp.int32)


def touch_ends(result, own_key, smallest, largest):
    place = [jax.random.randint(jax.random.fold_in(own_key, axis), (), 0, length) for axis, length in enumerate(result.shape)]
    main_axis = result.shape.index(max(result.shape))
    beside = place[:main_axis] + [(place[main_axis] + 1) % result.shape[main_axis]] + place[main_axis + 1:]
    return result.at[tuple(place)].set(smallest).at[tuple(beside)].set(largest)


def level_of(own_key, dims, split, least, largest):
    def one(position, blocks):
        heights = jax.random.uniform(jax.random.fold_in(jax.random.fold_in(own_key, 6), position), (blocks,), jnp.float32, least / len(split), largest / len(split))
        return jnp.repeat(jnp.exp(heights), dims[position] // blocks).reshape((-1,) + (1,) * (len(dims) - position - 1))

    level = one(*split[0])
    for cut in split[1:]:
        level = level * one(*cut)
    return level


def normal_values(own_key, extent, deviation, bound, cuts=(), kind=jnp.bfloat16):
    values = jax.random.normal(own_key, extent, jnp.float32) * deviation
    if len(cuts) > 0:
        values = level_of(own_key, extent, cuts, -0.22, 0.18) * values
    return jnp.clip(values, min=-bound, max=bound).astype(kind)


def setup_inputs(seed: int = 0) -> dict:
    key_list = jax.random.split(jax.random.key(seed), 8)
    amplitudes = normal_values(key_list[0], (ROWS, CD), 1.0, 6.0, ((0, 8), (1, 4)))
    amp_tiles = draw_amp_tiles(jax.random.fold_in(key_list[7], 71), 0)
    cd_width = touch_ends(jax.random.randint(key_list[2], (N_BLK,), TILE // 2, TILE + 1), jax.random.fold_in(key_list[2], 1), TILE // 2, TILE).astype(jnp.int32)
    integrals = normal_values(key_list[3], (N_GRP, TILE, AB), (TILE * N_BLK) ** -0.5, 0.25, ((0, 8), (2, 4)))
    int_tiles = touch_ends((jax.random.randint(key_list[4], (N_GRP, AT * N_BLK), 0, 4) < 3).astype(jnp.int32), jax.random.fold_in(key_list[4], 1), 0, 1)
    ab_width = touch_ends(jax.random.randint(key_list[5], (AT * N_BLK,), TILE // 2, TILE + 1), jax.random.fold_in(key_list[5], 1), TILE // 2, TILE).astype(jnp.int32)
    owners = draw_owners(jax.random.fold_in(key_list[7], 71), 0)
    return dict(amplitudes=amplitudes, amp_tiles=amp_tiles, cd_width=cd_width, integrals=integrals, int_tiles=int_tiles, ab_width=ab_width, owners=owners)


def reference(amplitudes, amp_tiles, cd_width, integrals, int_tiles, ab_width, owners):
    within_tile = jnp.arange(TILE)
    zero_value = jnp.zeros((), jnp.bfloat16)
    tiled_amps = amplitudes.reshape(ROWS // TILE, TILE, N_BLK, TILE)
    keep_amp = (amp_tiles[:, None, :, None] > 0) & (within_tile[None, None, None, :] < cd_width[None, None, :, None])
    masked_amps = jnp.where(keep_amp, tiled_amps, zero_value).reshape(ROWS, N_BLK * TILE)
    ab_tiles = AB // TILE
    tiled_ints = integrals.reshape(N_GRP, TILE, ab_tiles, TILE)
    masked_ints = jnp.where(int_tiles[:, None, :, None] > 0, tiled_ints, zero_value).reshape(N_GRP, TILE, AB)
    chosen = jnp.take(masked_ints, owners, axis=0).reshape(N_BLK * TILE, AB)
    column_keep = (within_tile[None, :] < ab_width[:, None]).reshape(AB)
    panel_width = AT * TILE
    results = []
    for block_idx in range(N_BLK):
        int_panel = chosen[:, block_idx * panel_width:(block_idx + 1) * panel_width]
        running = jnp.dot(masked_amps, int_panel, preferred_element_type=jnp.float32)
        keep_here = column_keep[block_idx * panel_width:(block_idx + 1) * panel_width]
        results.append(jnp.where(keep_here[None, :], 0.5 * running, 0.0).astype(jnp.bfloat16))
    return jnp.concatenate(results, axis=1)
```

```python
import functools

import jax
import jax.numpy as jnp
from jax import lax
from jax.experimental import pallas as pl
from jax.experimental.pallas import tpu as pltpu
from jax.sharding import PartitionSpec as P

UP, DOWN, PAIR = 0, 1, 2


class Gather:
    def __init__(self, axis, count, own, slot_of, send_sem, recv_sem):
        me = lax.axis_index(axis)
        self.axis, self.half = axis, count // 2
        self.pos, self.side = me // 2, me % 2
        self.own, self.slot_of = own, slot_of
        self.send_sem, self.recv_sem = send_sem, recv_sem
        self.not_last = self.pos + 1 < self.half
        self.not_first = self.pos > 0
        self.up = {axis: jnp.minimum(self.pos + 1, self.half - 1) * 2 + self.side}
        self.down = {axis: jnp.maximum(self.pos - 1, 0) * 2 + self.side}
        self.pair = {axis: self.pos * 2 + 1 - self.side}

    def signal_all(self, barrier):
        def to(device):
            pl.semaphore_signal(
                barrier, inc=1, device_id=device, device_id_type=pl.DeviceIdType.MESH
            )

        to(self.pair)
        pl.when(self.not_last)(lambda: to(self.up))
        pl.when(self.not_first)(lambda: to(self.down))

    def neighbours(self):
        return 1 + self.not_last.astype(jnp.int32) + self.not_first.astype(jnp.int32)

    def copy(self, kind, p, src=None, side=None):
        slot = self.slot_of(p * 2 + (self.side if side is None else side))
        return pltpu.make_async_remote_copy(
            src_ref=slot if src is None else src,
            dst_ref=slot,
            send_sem=self.send_sem.at[kind, p],
            recv_sem=self.recv_sem.at[kind, p],
            device_id=(self.up, self.down, self.pair)[kind],
            device_id_type=pl.DeviceIdType.MESH,
        )

    def begin(self):
        pl.when(self.not_last)(lambda: self.copy(UP, self.pos, self.own).start())
        pl.when(self.not_first)(lambda: self.copy(DOWN, self.pos, self.own).start())
        self.copy(PAIR, self.pos, self.own).start()

    def steps(self, first, last):
        def step(s, carry):
            below, above = self.pos - 1 - s, self.pos + 1 + s

            @pl.when(below >= 0)
            def _():
                self.copy(UP, below).wait_recv()
                pl.when(self.not_last)(lambda: self.copy(UP, below).start())
                self.copy(PAIR, below).start()

            @pl.when(above < self.half)
            def _():
                self.copy(DOWN, above).wait_recv()
                pl.when(self.not_first)(lambda: self.copy(DOWN, above).start())
                self.copy(PAIR, above).start()

            return carry

        lax.fori_loop(first, last, step, 0)

    def finish(self):
        def one(p, carry):
            self.copy(PAIR, p, side=1 - self.side).wait_recv()
            self.copy(PAIR, p).wait_send()

            @pl.when(self.not_last & (p <= self.pos))
            def _():
                self.copy(UP, p).wait_send()

            @pl.when(self.not_first & (p >= self.pos))
            def _():
                self.copy(DOWN, p).wait_send()

            return carry

        lax.fori_loop(0, self.half, one, 0)


def gather_kernel(
    groups, blocks, amps, amp_tiles, cd_width, ints, int_tiles,
    panels_out, amps_out, own_panel, own_amps, panel_send, panel_recv, amp_send, amp_recv, local,
):
    rows, tile = amps.shape
    width = ints.shape[2]
    panels = Gather("grp", groups, own_panel, lambda i: panels_out.at[i], panel_send, panel_recv)
    amplitudes = Gather(
        "blk", blocks, own_amps,
        lambda i: amps_out.at[:, pl.ds(pl.multiple_of(i * tile, tile), tile)],
        amp_send, amp_recv,
    )
    barrier = pltpu.get_barrier_semaphore()
    panels.signal_all(barrier)
    amplitudes.signal_all(barrier)

    for j in range(width // tile):
        cols = slice(j * tile, (j + 1) * tile)
        keep = jnp.full((tile, tile), int_tiles[0, j], jnp.int32) > 0
        own_panel[:, cols] = jnp.where(keep, ints[0, :, cols].astype(jnp.float32), 0.0).astype(
            jnp.bfloat16
        )
    pl.semaphore_wait(barrier, panels.neighbours() + amplitudes.neighbours())
    panels.begin()

    within = lax.broadcasted_iota(jnp.int32, (tile, tile), 1) < cd_width[0]
    for r in range(rows // tile):
        part = slice(r * tile, (r + 1) * tile)
        keep = (jnp.full((tile, tile), amp_tiles[r, 0], jnp.int32) > 0) & within
        own_amps[part, :] = jnp.where(keep, amps[part, :].astype(jnp.float32), 0.0).astype(
            jnp.bfloat16
        )
    amplitudes.begin()

    keep_panel = pltpu.make_async_copy(
        own_panel, panels_out.at[lax.axis_index("grp")], local.at[0]
    )
    keep_amps = pltpu.make_async_copy(
        own_amps, amplitudes.slot_of(lax.axis_index("blk")), local.at[1]
    )
    keep_panel.start()
    keep_amps.start()
    panels.steps(0, 1)
    amplitudes.steps(0, blocks // 2 - 1)
    panels.steps(1, groups // 2 - 1)
    amplitudes.finish()
    panels.finish()
    keep_panel.wait()
    keep_amps.wait()


def multiply_kernel(owners, ab_width, amps, panels, out, chosen, sem):
    tile = panels.shape[1]
    count = chosen.shape[0] // tile

    @pl.when(pl.program_id(0) == 0)
    def _():
        copies = [
            pltpu.make_async_copy(
                panels.at[owners[t]], chosen.at[pl.ds(t * tile, tile)], sem.at[t]
            )
            for t in range(count)
        ]
        for copy in copies:
            copy.start()
        for copy in copies:
            copy.wait()

    column = lax.broadcasted_iota(jnp.int32, (out.shape[0], 2 * tile), 1)
    for j in range(0, out.shape[1] // tile, 2):
        cols = slice(j * tile, (j + 2) * tile)
        total = jnp.dot(amps[...], chosen[:, cols], preferred_element_type=jnp.float32)
        limit = jnp.where(column < tile, ab_width[j], tile + ab_width[j + 1])
        out[:, cols] = jnp.where(column < limit, 0.5 * total, 0.0).astype(out.dtype)


def per_device(amplitudes, amp_tiles, cd_width, integrals, int_tiles, ab_width, owners):
    rows, tile = amplitudes.shape
    width = integrals.shape[2]
    groups, blocks = lax.axis_size("grp"), lax.axis_size("blk")
    vmem = pl.BlockSpec(memory_space=pltpu.VMEM)
    smem = pl.BlockSpec(memory_space=pltpu.SMEM)
    anywhere = pl.BlockSpec(memory_space=pl.ANY)
    panels, amps = pl.pallas_call(
        functools.partial(gather_kernel, groups, blocks),
        out_shape=(
            jax.ShapeDtypeStruct((groups, tile, width), jnp.bfloat16),
            jax.ShapeDtypeStruct((rows, blocks * tile), jnp.bfloat16),
        ),
        in_specs=[vmem, smem, smem, vmem, smem],
        out_specs=(anywhere, anywhere),
        scratch_shapes=[
            pltpu.VMEM((tile, width), jnp.bfloat16),
            pltpu.VMEM((rows, tile), jnp.bfloat16),
            pltpu.SemaphoreType.DMA((3, groups // 2)),
            pltpu.SemaphoreType.DMA((3, groups // 2)),
            pltpu.SemaphoreType.DMA((3, blocks // 2)),
            pltpu.SemaphoreType.DMA((3, blocks // 2)),
            pltpu.SemaphoreType.DMA((2,)),
        ],
        compiler_params=pltpu.CompilerParams(
            collective_id=0, has_side_effects=True, vmem_limit_bytes=16 * 2**20
        ),
    )(amplitudes, amp_tiles, cd_width, integrals, int_tiles)
    step = 256
    return pl.pallas_call(
        multiply_kernel,
        out_shape=jax.ShapeDtypeStruct((rows, width), jnp.bfloat16),
        grid=(rows // step,),
        in_specs=[smem, smem, pl.BlockSpec((step, blocks * tile), lambda i: (i, 0)), anywhere],
        out_specs=pl.BlockSpec((step, width), lambda i: (i, 0)),
        scratch_shapes=[
            pltpu.VMEM((blocks * tile, width), jnp.bfloat16),
            pltpu.SemaphoreType.DMA((blocks,)),
        ],
        compiler_params=pltpu.CompilerParams(vmem_limit_bytes=16 * 2**20),
    )(owners, ab_width, amps, panels)


def solution(mesh):
    placed = (
        P("grp", "blk"),
        P("grp", "blk"),
        P("blk"),
        P("grp", None, "blk"),
        P("grp", "blk"),
        P("blk"),
        P(),
    )
    return jax.shard_map(
        per_device, mesh=mesh, in_specs=placed, out_specs=P("grp", "blk"), check_vma=False
    )
```

```python
import functools

import jax
import jax.numpy as jnp
from jax import lax
from jax.experimental import pallas as pl
from jax.experimental.pallas import tpu as pltpu
from jax.sharding import PartitionSpec as P

UP, DOWN, PAIR = 0, 1, 2


class Gather:
    def __init__(self, axis, count, own, slot_of, send_sem, recv_sem):
        me = lax.axis_index(axis)
        self.axis, self.half = axis, count // 2
        self.pos, self.side = me // 2, me % 2
        self.own, self.slot_of = own, slot_of
        self.send_sem, self.recv_sem = send_sem, recv_sem
        self.not_last = self.pos + 1 < self.half
        self.not_first = self.pos > 0
        self.up = {axis: jnp.minimum(self.pos + 1, self.half - 1) * 2 + self.side}
        self.down = {axis: jnp.maximum(self.pos - 1, 0) * 2 + self.side}
        self.pair = {axis: self.pos * 2 + 1 - self.side}

    def signal_all(self, barrier):
        def to(device):
            pl.semaphore_signal(
                barrier, inc=1, device_id=device, device_id_type=pl.DeviceIdType.MESH
            )

        to(self.pair)
        pl.when(self.not_last)(lambda: to(self.up))
        pl.when(self.not_first)(lambda: to(self.down))

    def neighbours(self):
        return 1 + self.not_last.astype(jnp.int32) + self.not_first.astype(jnp.int32)

    def copy(self, kind, p, src=None, side=None):
        slot = self.slot_of(p * 2 + (self.side if side is None else side))
        return pltpu.make_async_remote_copy(
            src_ref=slot if src is None else src,
            dst_ref=slot,
            send_sem=self.send_sem.at[kind, p],
            recv_sem=self.recv_sem.at[kind, p],
            device_id=(self.up, self.down, self.pair)[kind],
            device_id_type=pl.DeviceIdType.MESH,
        )

    def begin(self):
        pl.when(self.not_last)(lambda: self.copy(UP, self.pos, self.own).start())
        pl.when(self.not_first)(lambda: self.copy(DOWN, self.pos, self.own).start())
        self.copy(PAIR, self.pos, self.own).start()

    def steps(self, first, last):
        def step(s, carry):
            below, above = self.pos - 1 - s, self.pos + 1 + s

            @pl.when(below >= 0)
            def _():
                self.copy(UP, below).wait_recv()
                pl.when(self.not_last)(lambda: self.copy(UP, below).start())
                self.copy(PAIR, below).start()

            @pl.when(above < self.half)
            def _():
                self.copy(DOWN, above).wait_recv()
                pl.when(self.not_first)(lambda: self.copy(DOWN, above).start())
                self.copy(PAIR, above).start()

            return carry

        lax.fori_loop(first, last, step, 0)

    def finish(self):
        def one(p, carry):
            self.copy(PAIR, p, side=1 - self.side).wait_recv()
            self.copy(PAIR, p).wait_send()

            @pl.when(self.not_last & (p <= self.pos))
            def _():
                self.copy(UP, p).wait_send()

            @pl.when(self.not_first & (p >= self.pos))
            def _():
                self.copy(DOWN, p).wait_send()

            return carry

        lax.fori_loop(0, self.half, one, 0)


def ladder_kernel(
    groups, blocks, amps, amp_tiles, cd_width, ints, int_tiles, ab_width, owners, out,
    panels, all_amps, own_panel, own_amps, amp_tiles_s, cd_width_s, int_tiles_s, ab_width_s,
    owners_s, panel_send, panel_recv, amp_send, amp_recv, local, result, out_sem,
):
    rows, tile = own_amps.shape
    width = own_panel.shape[1]
    fetches = [
        pltpu.make_async_copy(source, target, local.at[i])
        for i, (source, target) in enumerate(
            (
                (int_tiles, int_tiles_s),
                (ints.at[0], own_panel),
                (amp_tiles, amp_tiles_s),
                (cd_width, cd_width_s),
                (amps, own_amps),
                (ab_width, ab_width_s),
                (owners, owners_s),
            )
        )
    ]
    for fetch in fetches:
        fetch.start()
    panel_gather = Gather(
        "grp", groups, own_panel, lambda i: panels.at[i], panel_send, panel_recv
    )
    amp_gather = Gather(
        "blk", blocks, own_amps,
        lambda i: all_amps.at[:, pl.ds(pl.multiple_of(i * tile, tile), tile)],
        amp_send, amp_recv,
    )
    barrier = pltpu.get_barrier_semaphore()
    panel_gather.signal_all(barrier)
    amp_gather.signal_all(barrier)

    fetches[0].wait()
    fetches[1].wait()
    for j in range(width // tile):
        cols = slice(j * tile, (j + 1) * tile)
        keep = jnp.full((tile, tile), int_tiles_s[0, j], jnp.int32) > 0
        own_panel[:, cols] = jnp.where(
            keep, own_panel[:, cols].astype(jnp.float32), 0.0
        ).astype(jnp.bfloat16)
    for fetch in fetches[2:5]:
        fetch.wait()
    within = lax.broadcasted_iota(jnp.int32, (tile, tile), 1) < cd_width_s[0]
    for r in range(rows // tile):
        part = slice(r * tile, (r + 1) * tile)
        keep = (jnp.full((tile, tile), amp_tiles_s[0, r], jnp.int32) > 0) & within
        own_amps[part, :] = jnp.where(keep, own_amps[part, :].astype(jnp.float32), 0.0).astype(
            jnp.bfloat16
        )
    pl.semaphore_wait(barrier, panel_gather.neighbours() + amp_gather.neighbours())
    panel_gather.begin()
    amp_gather.begin()

    panels[lax.axis_index("grp")] = own_panel[...]
    mine = pl.multiple_of(lax.axis_index("blk") * tile, tile)
    all_amps[:, pl.ds(mine, tile)] = own_amps[...]
    panel_gather.steps(0, 1)
    amp_gather.steps(0, blocks // 2 - 1)
    panel_gather.steps(1, groups // 2 - 1)
    amp_gather.finish()
    fetches[5].wait()
    fetches[6].wait()
    panel_gather.finish()

    column = lax.broadcasted_iota(jnp.int32, (rows, 2 * tile), 1)

    def store(j):
        cols = pl.ds(pl.multiple_of(j * 2 * tile, 2 * tile), 2 * tile)
        return pltpu.make_async_copy(result.at[:, cols], out.at[:, cols], out_sem.at[j])

    def columns(j, carry):
        cols = pl.ds(pl.multiple_of(j * 2 * tile, 2 * tile), 2 * tile)
        chosen = jnp.concatenate([panels[owners_s[t], :, cols] for t in range(blocks)], axis=0)
        total = jnp.dot(all_amps[...], chosen, preferred_element_type=jnp.float32)
        limit = jnp.where(column < tile, ab_width_s[2 * j], tile + ab_width_s[2 * j + 1])
        result[:, cols] = jnp.where(column < limit, 0.5 * total, 0.0).astype(out.dtype)
        store(j).start()
        return carry

    count = width // (2 * tile)
    lax.fori_loop(0, count, columns, 0)
    lax.fori_loop(0, count, lambda j, carry: (store(j).wait(), carry)[1], 0)


def per_device(amplitudes, amp_tiles, cd_width, integrals, int_tiles, ab_width, owners):
    rows, tile = amplitudes.shape
    width = integrals.shape[2]
    groups, blocks = lax.axis_size("grp"), lax.axis_size("blk")
    hbm = pl.BlockSpec(memory_space=pltpu.HBM)
    amp_tiles = amp_tiles.T
    return pl.pallas_call(
        functools.partial(ladder_kernel, groups, blocks),
        out_shape=jax.ShapeDtypeStruct((rows, width), jnp.bfloat16),
        in_specs=[hbm] * 7,
        out_specs=hbm,
        scratch_shapes=[
            pltpu.VMEM((groups, tile, width), jnp.bfloat16),
            pltpu.VMEM((rows, blocks * tile), jnp.bfloat16),
            pltpu.VMEM((tile, width), jnp.bfloat16),
            pltpu.VMEM((rows, tile), jnp.bfloat16),
            pltpu.SMEM(amp_tiles.shape, jnp.int32),
            pltpu.SMEM(cd_width.shape, jnp.int32),
            pltpu.SMEM(int_tiles.shape, jnp.int32),
            pltpu.SMEM(ab_width.shape, jnp.int32),
            pltpu.SMEM(owners.shape, jnp.int32),
            pltpu.SemaphoreType.DMA((3, groups // 2)),
            pltpu.SemaphoreType.DMA((3, groups // 2)),
            pltpu.SemaphoreType.DMA((3, blocks // 2)),
            pltpu.SemaphoreType.DMA((3, blocks // 2)),
            pltpu.SemaphoreType.DMA((7,)),
            pltpu.VMEM((rows, width), jnp.bfloat16),
            pltpu.SemaphoreType.DMA((width // (2 * tile),)),
        ],
        compiler_params=pltpu.CompilerParams(
            collective_id=0,
            has_side_effects=True,
            vmem_limit_bytes=60 * 2**20,
        ),
    )(amplitudes, amp_tiles, cd_width, integrals, int_tiles, ab_width, owners)


def solution(mesh):
    placed = (
        P("grp", "blk"),
        P("grp", "blk"),
        P("blk"),
        P("grp", None, "blk"),
        P("grp", "blk"),
        P("blk"),
        P(),
    )
    return jax.shard_map(
        per_device, mesh=mesh, in_specs=placed, out_specs=P("grp", "blk"), check_vma=False
    )
```

```python
import functools

import jax
import jax.numpy as jnp
from jax import lax
from jax.experimental import pallas as pl
from jax.experimental.pallas import tpu as pltpu
from jax.sharding import PartitionSpec as P

UP, DOWN, PAIR, CROSSED = 0, 1, 2, 3


class Gather:
    def __init__(self, axis, count, split, own, slot_of, send_sem, recv_sem):
        me = lax.axis_index(axis)
        self.half, self.split = count // 2, split
        self.pos, self.side = me // 2, me % 2
        self.own, self.slot_of = own, slot_of
        self.send_sem, self.recv_sem = send_sem, recv_sem
        self.not_last = self.pos + 1 < self.half
        self.not_first = self.pos > 0
        self.up = {axis: jnp.minimum(self.pos + 1, self.half - 1) * 2 + self.side}
        self.down = {axis: jnp.maximum(self.pos - 1, 0) * 2 + self.side}
        self.pair = {axis: self.pos * 2 + 1 - self.side}

    def signal_all(self, barrier):
        def to(device):
            pl.semaphore_signal(
                barrier, inc=1, device_id=device, device_id_type=pl.DeviceIdType.MESH
            )

        to(self.pair)
        pl.when(self.not_last)(lambda: to(self.up))
        pl.when(self.not_first)(lambda: to(self.down))

    def neighbours(self):
        return 1 + self.not_last.astype(jnp.int32) + self.not_first.astype(jnp.int32)

    def copy(self, kind, h, p, own=False, other=False):
        slot = self.slot_of(p * 2 + (1 - self.side if other else self.side), h)
        row = kind * 2 + h if kind < CROSSED else 2 * CROSSED + h
        target = (self.up, self.down, self.pair, (self.up, self.down)[h])[kind]
        if kind == CROSSED:
            slot = self.slot_of(p * 2 + 1 - self.side, 0)
        return pltpu.make_async_remote_copy(
            src_ref=self.own(h) if own else slot,
            dst_ref=slot,
            send_sem=self.send_sem.at[row, p],
            recv_sem=self.recv_sem.at[row, p],
            device_id=target,
            device_id_type=pl.DeviceIdType.MESH,
        )

    def cross(self, p):
        return self.split & ((p == 0) | (p == self.half - 1))

    def begin(self):
        for h in (0, 1):
            self.copy(PAIR, h, self.pos, own=True).start()
        for h in (1, 0):
            pl.when(self.not_last)(lambda h=h: self.copy(UP, h, self.pos, own=True).start())
            pl.when(self.not_first)(lambda h=h: self.copy(DOWN, h, self.pos, own=True).start())

    def begin_crossed(self):
        for way, end, last in ((UP, 0, self.half - 1), (DOWN, self.half - 1, 0)):

            @pl.when(self.pos == end)
            def _(way=way, end=end):
                self.copy(PAIR, 0, end, other=True).wait_recv()
                self.copy(CROSSED, way, end).start()

    def steps(self, first, last):
        def arrived(way, p, going_on, end):
            for h in (1, 0):
                self.copy(way, h, p).wait_recv()
                pl.when(going_on)(lambda h=h: self.copy(way, h, p).start())
                if h == 1 or not self.split:
                    self.copy(PAIR, h, p).start()
                else:
                    pl.when(jnp.logical_not(self.cross(p)))(
                        lambda h=h: self.copy(PAIR, h, p).start()
                    )
            if self.split:

                @pl.when(p == end)
                def _():
                    self.copy(CROSSED, way, end).wait_recv()
                    pl.when(going_on)(lambda: self.copy(CROSSED, way, end).start())

        def step(s, carry):
            below, above = self.pos - 1 - s, self.pos + 1 + s
            pl.when(below >= 0)(lambda: arrived(UP, below, self.not_last, 0))
            pl.when(above < self.half)(
                lambda: arrived(DOWN, above, self.not_first, self.half - 1)
            )
            return carry

        lax.fori_loop(first, last, step, 0)

    def finish(self):
        def one(p, carry):
            self.copy(PAIR, 1, p, other=True).wait_recv()
            self.copy(PAIR, 1, p).wait_send()
            if self.split:

                @pl.when(jnp.logical_not(self.cross(p)))
                def _():
                    self.copy(PAIR, 0, p, other=True).wait_recv()
                    self.copy(PAIR, 0, p).wait_send()

                @pl.when(self.cross(p) & (p == self.pos))
                def _():
                    self.copy(PAIR, 0, p).wait_send()

            else:
                self.copy(PAIR, 0, p, other=True).wait_recv()
                self.copy(PAIR, 0, p).wait_send()

            @pl.when(self.not_last & (p <= self.pos))
            def _():
                for h in (0, 1):
                    self.copy(UP, h, p).wait_send()

            @pl.when(self.not_first & (p >= self.pos))
            def _():
                for h in (0, 1):
                    self.copy(DOWN, h, p).wait_send()

            return carry

        lax.fori_loop(0, self.half, one, 0)
        if self.split:
            pl.when(self.not_last)(lambda: self.copy(CROSSED, UP, 0).wait_send())
            pl.when(self.not_first)(lambda: self.copy(CROSSED, DOWN, self.half - 1).wait_send())


def gather_kernel(
    groups, blocks, amps, amp_tiles, cd_width, ints, int_tiles, panels, all_amps,
    own_panel, own_amps, amp_tiles_s, cd_width_s, int_tiles_s,
    panel_send, panel_recv, amp_send, amp_recv, local,
):
    rows, tile = own_amps.shape
    width = own_panel.shape[1]
    fetches = [
        pltpu.make_async_copy(source, target, local.at[i])
        for i, (source, target) in enumerate(
            (
                (int_tiles, int_tiles_s),
                (ints.at[0], own_panel),
                (amp_tiles, amp_tiles_s),
                (cd_width, cd_width_s),
                (amps, own_amps),
            )
        )
    ]
    for fetch in fetches:
        fetch.start()
    panel_gather = Gather(
        "grp", groups, True,
        lambda h: own_panel.at[pl.ds(h * (tile // 2), tile // 2)],
        lambda i, h: panels.at[i, pl.ds(h * (tile // 2), tile // 2)],
        panel_send, panel_recv,
    )
    amp_gather = Gather(
        "blk", blocks, False,
        lambda h: own_amps.at[pl.ds(h * (rows // 2), rows // 2)],
        lambda i, h: all_amps.at[
            pl.ds(h * (rows // 2), rows // 2), pl.ds(pl.multiple_of(i * tile, tile), tile)
        ],
        amp_send, amp_recv,
    )
    barrier = pltpu.get_barrier_semaphore()
    panel_gather.signal_all(barrier)
    amp_gather.signal_all(barrier)

    fetches[0].wait()
    fetches[1].wait()
    for j in range(width // tile):
        cols = slice(j * tile, (j + 1) * tile)
        keep = jnp.full((tile, tile), int_tiles_s[0, j], jnp.int32) > 0
        own_panel[:, cols] = jnp.where(
            keep, own_panel[:, cols].astype(jnp.float32), 0.0
        ).astype(jnp.bfloat16)
    for fetch in fetches[2:]:
        fetch.wait()
    within = lax.broadcasted_iota(jnp.int32, (tile, tile), 1) < cd_width_s[0]
    for r in range(rows // tile):
        part = slice(r * tile, (r + 1) * tile)
        keep = (jnp.full((tile, tile), amp_tiles_s[0, r], jnp.int32) > 0) & within
        own_amps[part, :] = jnp.where(keep, own_amps[part, :].astype(jnp.float32), 0.0).astype(
            jnp.bfloat16
        )
    pl.semaphore_wait(barrier, panel_gather.neighbours() + amp_gather.neighbours())
    panel_gather.begin()
    amp_gather.begin()
    mine = pl.ds(pl.multiple_of(lax.axis_index("blk") * tile, tile), tile)
    keeps = [
        pltpu.make_async_copy(own_panel, panels.at[lax.axis_index("grp")], local.at[0]),
        pltpu.make_async_copy(own_amps, all_amps.at[:, mine], local.at[1]),
    ]
    for keep in keeps:
        keep.start()
    panel_gather.begin_crossed()
    panel_gather.steps(0, 1)
    amp_gather.steps(0, blocks // 2 - 1)
    panel_gather.steps(1, groups // 2 - 1)
    for keep in keeps:
        keep.wait()
    amp_gather.finish()
    panel_gather.finish()


def multiply_kernel(
    owners, ab_width, amps, panels, out, owners_s, ab_width_s, all_amps, chosen, result, sem, cut_sem, out_sem
):
    tile = panels.shape[1]
    rows, width = out.shape
    step = 2 * tile
    count = chosen.shape[0] // tile
    fetches = [
        pltpu.make_async_copy(source, target, sem.at[i])
        for i, (source, target) in enumerate(
            ((owners, owners_s), (ab_width, ab_width_s), (amps, all_amps))
        )
    ]
    for fetch in fetches:
        fetch.start()
    fetches[0].wait()
    pieces = [
        [
            pltpu.make_async_copy(
                panels.at[owners_s[t], :, pl.ds(j * step, step)],
                chosen.at[pl.ds(t * tile, tile), pl.ds(j * step, step)],
                cut_sem.at[j, t],
            )
            for t in range(count)
        ]
        for j in range(width // step)
    ]
    for cut in pieces:
        for piece in cut:
            piece.start()
    fetches[1].wait()
    fetches[2].wait()
    column = lax.broadcasted_iota(jnp.int32, (rows, step), 1)
    stores = []
    for j, cut in enumerate(pieces):
        for piece in cut:
            piece.wait()
        cols = slice(j * step, (j + 1) * step)
        total = jnp.dot(all_amps[...], chosen[:, cols], preferred_element_type=jnp.float32)
        limit = jnp.where(column < tile, ab_width_s[2 * j], tile + ab_width_s[2 * j + 1])
        result[:, cols] = jnp.where(column < limit, 0.5 * total, 0.0).astype(out.dtype)
        store = pltpu.make_async_copy(
            result.at[:, pl.ds(j * step, step)], out.at[:, pl.ds(j * step, step)], out_sem.at[j]
        )
        store.start()
        stores.append(store)
    for store in stores:
        store.wait()


def per_device(amplitudes, amp_tiles, cd_width, integrals, int_tiles, ab_width, owners):
    rows, tile = amplitudes.shape
    width = integrals.shape[2]
    groups, blocks = lax.axis_size("grp"), lax.axis_size("blk")
    hbm = pl.BlockSpec(memory_space=pltpu.HBM)
    amp_tiles = amp_tiles.T
    limit = 60 * 2**20
    panels, amps = pl.pallas_call(
        functools.partial(gather_kernel, groups, blocks),
        out_shape=(
            jax.ShapeDtypeStruct((groups, tile, width), jnp.bfloat16),
            jax.ShapeDtypeStruct((rows, blocks * tile), jnp.bfloat16),
        ),
        in_specs=[hbm] * 5,
        out_specs=(hbm, hbm),
        scratch_shapes=[
            pltpu.VMEM((tile, width), jnp.bfloat16),
            pltpu.VMEM((rows, tile), jnp.bfloat16),
            pltpu.SMEM(amp_tiles.shape, jnp.int32),
            pltpu.SMEM(cd_width.shape, jnp.int32),
            pltpu.SMEM(int_tiles.shape, jnp.int32),
            pltpu.SemaphoreType.DMA((8, groups // 2)),
            pltpu.SemaphoreType.DMA((8, groups // 2)),
            pltpu.SemaphoreType.DMA((8, blocks // 2)),
            pltpu.SemaphoreType.DMA((8, blocks // 2)),
            pltpu.SemaphoreType.DMA((5,)),
        ],
        compiler_params=pltpu.CompilerParams(
            collective_id=0, has_side_effects=True, vmem_limit_bytes=limit
        ),
    )(amplitudes, amp_tiles, cd_width, integrals, int_tiles)
    cuts = width // (2 * tile)
    return pl.pallas_call(
        multiply_kernel,
        out_shape=jax.ShapeDtypeStruct((rows, width), jnp.bfloat16),
        in_specs=[hbm] * 4,
        out_specs=hbm,
        scratch_shapes=[
            pltpu.SMEM(owners.shape, jnp.int32),
            pltpu.SMEM(ab_width.shape, jnp.int32),
            pltpu.VMEM((rows, blocks * tile), jnp.bfloat16),
            pltpu.VMEM((blocks * tile, width), jnp.bfloat16),
            pltpu.VMEM((rows, width), jnp.bfloat16),
            pltpu.SemaphoreType.DMA((3,)),
            pltpu.SemaphoreType.DMA((cuts, blocks)),
            pltpu.SemaphoreType.DMA((cuts,)),
        ],
        compiler_params=pltpu.CompilerParams(vmem_limit_bytes=limit),
    )(owners, ab_width, amps, panels)


def solution(mesh):
    placed = (
        P("grp", "blk"),
        P("grp", "blk"),
        P("blk"),
        P("grp", None, "blk"),
        P("grp", "blk"),
        P("blk"),
        P(),
    )
    return jax.shard_map(
        per_device, mesh=mesh, in_specs=placed, out_specs=P("grp", "blk"), check_vma=False
    )
```

```python
import functools

import jax
import jax.numpy as jnp
from jax import lax
from jax.experimental import pallas as pl
from jax.experimental.pallas import tpu as pltpu
from jax.sharding import PartitionSpec as P

UP, DOWN, PAIR, CROSSED = 0, 1, 2, 3


class Gather:
    def __init__(self, axis, count, split, own, slot_of, send_sem, recv_sem):
        me = lax.axis_index(axis)
        self.half, self.split = count // 2, split
        self.pos, self.side = me // 2, me % 2
        self.own, self.slot_of = own, slot_of
        self.send_sem, self.recv_sem = send_sem, recv_sem
        self.not_last = self.pos + 1 < self.half
        self.not_first = self.pos > 0
        self.up = {axis: jnp.minimum(self.pos + 1, self.half - 1) * 2 + self.side}
        self.down = {axis: jnp.maximum(self.pos - 1, 0) * 2 + self.side}
        self.pair = {axis: self.pos * 2 + 1 - self.side}

    def signal_all(self, barrier):
        def to(device):
            pl.semaphore_signal(
                barrier, inc=1, device_id=device, device_id_type=pl.DeviceIdType.MESH
            )

        to(self.pair)
        pl.when(self.not_last)(lambda: to(self.up))
        pl.when(self.not_first)(lambda: to(self.down))

    def neighbours(self):
        return 1 + self.not_last.astype(jnp.int32) + self.not_first.astype(jnp.int32)

    def copy(self, kind, h, p, own=False, other=False):
        slot = self.slot_of(p * 2 + (1 - self.side if other else self.side), h)
        row = kind * 2 + h if kind < CROSSED else 2 * CROSSED + h
        target = (self.up, self.down, self.pair, (self.up, self.down)[h])[kind]
        if kind == CROSSED:
            slot = self.slot_of(p * 2 + 1 - self.side, 0)
        return pltpu.make_async_remote_copy(
            src_ref=self.own(h) if own else slot,
            dst_ref=slot,
            send_sem=self.send_sem.at[row, p],
            recv_sem=self.recv_sem.at[row, p],
            device_id=target,
            device_id_type=pl.DeviceIdType.MESH,
        )

    def cross(self, p):
        return self.split & ((p == 0) | (p == self.half - 1))

    def begin(self):
        for h in (0, 1):
            self.copy(PAIR, h, self.pos, own=True).start()
        for h in (1, 0):
            pl.when(self.not_last)(lambda h=h: self.copy(UP, h, self.pos, own=True).start())
            pl.when(self.not_first)(lambda h=h: self.copy(DOWN, h, self.pos, own=True).start())

    def begin_crossed(self):
        for way, end, last in ((UP, 0, self.half - 1), (DOWN, self.half - 1, 0)):

            @pl.when(self.pos == end)
            def _(way=way, end=end):
                self.copy(PAIR, 0, end, other=True).wait_recv()
                self.copy(CROSSED, way, end).start()

    def steps(self, first, last):
        def arrived(way, p, going_on, end):
            for h in (1, 0):
                self.copy(way, h, p).wait_recv()
                pl.when(going_on)(lambda h=h: self.copy(way, h, p).start())
                if h == 1 or not self.split:
                    self.copy(PAIR, h, p).start()
                else:
                    pl.when(jnp.logical_not(self.cross(p)))(
                        lambda h=h: self.copy(PAIR, h, p).start()
                    )
            if self.split:

                @pl.when(p == end)
                def _():
                    self.copy(CROSSED, way, end).wait_recv()
                    pl.when(going_on)(lambda: self.copy(CROSSED, way, end).start())

        def step(s, carry):
            below, above = self.pos - 1 - s, self.pos + 1 + s
            pl.when(below >= 0)(lambda: arrived(UP, below, self.not_last, 0))
            pl.when(above < self.half)(
                lambda: arrived(DOWN, above, self.not_first, self.half - 1)
            )
            return carry

        lax.fori_loop(first, last, step, 0)

    def finish(self):
        def one(p, carry):
            self.copy(PAIR, 1, p, other=True).wait_recv()
            self.copy(PAIR, 1, p).wait_send()
            if self.split:

                @pl.when(jnp.logical_not(self.cross(p)))
                def _():
                    self.copy(PAIR, 0, p, other=True).wait_recv()
                    self.copy(PAIR, 0, p).wait_send()

                @pl.when(self.cross(p) & (p == self.pos))
                def _():
                    self.copy(PAIR, 0, p).wait_send()

            else:
                self.copy(PAIR, 0, p, other=True).wait_recv()
                self.copy(PAIR, 0, p).wait_send()

            @pl.when(self.not_last & (p <= self.pos))
            def _():
                for h in (0, 1):
                    self.copy(UP, h, p).wait_send()

            @pl.when(self.not_first & (p >= self.pos))
            def _():
                for h in (0, 1):
                    self.copy(DOWN, h, p).wait_send()

            return carry

        lax.fori_loop(0, self.half, one, 0)
        if self.split:
            pl.when(self.not_last)(lambda: self.copy(CROSSED, UP, 0).wait_send())
            pl.when(self.not_first)(lambda: self.copy(CROSSED, DOWN, self.half - 1).wait_send())


def gather_kernel(
    groups, blocks, amps, amp_tiles, cd_width, ints, int_tiles, panels, all_amps,
    own_panel, own_amps, amp_tiles_s, cd_width_s, int_tiles_s,
    panel_send, panel_recv, amp_send, amp_recv, local,
):
    rows, tile = own_amps.shape
    width = own_panel.shape[1]
    fetches = [
        pltpu.make_async_copy(source, target, local.at[i])
        for i, (source, target) in enumerate(
            (
                (int_tiles, int_tiles_s),
                (ints.at[0], own_panel),
                (amp_tiles, amp_tiles_s),
                (cd_width, cd_width_s),
                (amps, own_amps),
            )
        )
    ]
    for fetch in fetches:
        fetch.start()
    panel_gather = Gather(
        "grp", groups, True,
        lambda h: own_panel.at[pl.ds(h * (tile // 2), tile // 2)],
        lambda i, h: panels.at[i, pl.ds(h * (tile // 2), tile // 2)],
        panel_send, panel_recv,
    )
    amp_gather = Gather(
        "blk", blocks, False,
        lambda h: own_amps.at[pl.ds(h * (rows // 2), rows // 2)],
        lambda i, h: all_amps.at[
            pl.ds(h * (rows // 2), rows // 2), pl.ds(pl.multiple_of(i * tile, tile), tile)
        ],
        amp_send, amp_recv,
    )
    barrier = pltpu.get_barrier_semaphore()
    panel_gather.signal_all(barrier)
    amp_gather.signal_all(barrier)

    fetches[0].wait()
    fetches[1].wait()
    for j in range(width // tile):
        cols = slice(j * tile, (j + 1) * tile)
        keep = jnp.full((tile, tile), int_tiles_s[0, j], jnp.int32) > 0
        own_panel[:, cols] = jnp.where(
            keep, own_panel[:, cols].astype(jnp.float32), 0.0
        ).astype(jnp.bfloat16)
    pl.semaphore_wait(barrier, panel_gather.neighbours() + amp_gather.neighbours())
    panel_gather.begin()
    for fetch in fetches[2:]:
        fetch.wait()
    within = lax.broadcasted_iota(jnp.int32, (tile, tile), 1) < cd_width_s[0]
    for r in range(rows // tile):
        part = slice(r * tile, (r + 1) * tile)
        keep = (jnp.full((tile, tile), amp_tiles_s[0, r], jnp.int32) > 0) & within
        own_amps[part, :] = jnp.where(keep, own_amps[part, :].astype(jnp.float32), 0.0).astype(
            jnp.bfloat16
        )
    amp_gather.begin()
    mine = pl.ds(pl.multiple_of(lax.axis_index("blk") * tile, tile), tile)
    keeps = [
        pltpu.make_async_copy(own_panel, panels.at[lax.axis_index("grp")], local.at[0]),
        pltpu.make_async_copy(own_amps, all_amps.at[:, mine], local.at[1]),
    ]
    for keep in keeps:
        keep.start()
    panel_gather.begin_crossed()
    panel_gather.steps(0, 1)
    amp_gather.steps(0, blocks // 2 - 1)
    panel_gather.steps(1, groups // 2 - 1)
    for keep in keeps:
        keep.wait()
    amp_gather.finish()
    panel_gather.finish()


def multiply_kernel(
    owners, ab_width, amps, panels, out,
    owners_s, ab_width_s, all_amps, held, result, sem, held_sem, amp_sem, out_sem,
):
    tile = panels.shape[1]
    rows, width = out.shape
    count = owners.shape[0]
    part = rows // amp_sem.shape[0]
    whole = held.shape[0] == panels.shape[0]

    def rows_of(r):
        return pl.ds(pl.multiple_of(r * part, part), part)

    def fetch_amps(r):
        return pltpu.make_async_copy(
            amps.at[rows_of(r)], all_amps.at[rows_of(r)], amp_sem.at[r]
        )

    def store(r):
        return pltpu.make_async_copy(result.at[rows_of(r)], out.at[rows_of(r)], out_sem.at[r])

    scalars = [
        pltpu.make_async_copy(owners, owners_s, sem.at[0]),
        pltpu.make_async_copy(ab_width, ab_width_s, sem.at[1]),
    ]
    for fetch in scalars:
        fetch.start()
    if not whole:
        scalars[0].wait()
    fetches = [
        pltpu.make_async_copy(panels.at[i if whole else owners_s[i]], held.at[i], held_sem.at[i])
        for i in range(held.shape[0])
    ]
    for fetch in fetches:
        fetch.start()
    for r in range(rows // part):
        fetch_amps(r).start()
    if whole:
        scalars[0].wait()
    scalars[1].wait()
    for fetch in fetches:
        fetch.wait()
    column = lax.broadcasted_iota(jnp.int32, (1, 2 * tile), 1)

    def multiply(r, carry):
        fetch_amps(r).wait()
        for j in range(0, width // tile, 2):
            cols = slice(j * tile, (j + 2) * tile)
            chosen = jnp.concatenate(
                [held[owners_s[t] if whole else t, :, cols] for t in range(count)], axis=0
            )
            total = jnp.dot(
                all_amps[rows_of(r), :], chosen, preferred_element_type=jnp.float32
            )
            limit = jnp.where(column < tile, ab_width_s[j], tile + ab_width_s[j + 1])
            result[rows_of(r), cols] = jnp.where(column < limit, 0.5 * total, 0.0).astype(
                out.dtype
            )
        store(r).start()
        return carry

    parts = rows // part
    lax.fori_loop(0, parts, multiply, 0)
    lax.fori_loop(0, parts, lambda r, carry: (store(r).wait(), carry)[1], 0)


def per_device(amplitudes, amp_tiles, cd_width, integrals, int_tiles, ab_width, owners):
    rows, tile = amplitudes.shape
    width = integrals.shape[2]
    groups, blocks = lax.axis_size("grp"), lax.axis_size("blk")
    hbm = pl.BlockSpec(memory_space=pltpu.HBM)
    amp_tiles = amp_tiles.T
    limit = 60 * 2**20
    panels, amps = pl.pallas_call(
        functools.partial(gather_kernel, groups, blocks),
        out_shape=(
            jax.ShapeDtypeStruct((groups, tile, width), jnp.bfloat16),
            jax.ShapeDtypeStruct((rows, blocks * tile), jnp.bfloat16),
        ),
        in_specs=[hbm] * 5,
        out_specs=(hbm, hbm),
        scratch_shapes=[
            pltpu.VMEM((tile, width), jnp.bfloat16),
            pltpu.VMEM((rows, tile), jnp.bfloat16),
            pltpu.SMEM(amp_tiles.shape, jnp.int32),
            pltpu.SMEM(cd_width.shape, jnp.int32),
            pltpu.SMEM(int_tiles.shape, jnp.int32),
            pltpu.SemaphoreType.DMA((8, groups // 2)),
            pltpu.SemaphoreType.DMA((8, groups // 2)),
            pltpu.SemaphoreType.DMA((8, blocks // 2)),
            pltpu.SemaphoreType.DMA((8, blocks // 2)),
            pltpu.SemaphoreType.DMA((5,)),
        ],
        compiler_params=pltpu.CompilerParams(
            collective_id=0, has_side_effects=True, vmem_limit_bytes=limit
        ),
    )(amplitudes, amp_tiles, cd_width, integrals, int_tiles)
    held = groups if groups <= 2 * blocks else blocks
    return pl.pallas_call(
        multiply_kernel,
        out_shape=jax.ShapeDtypeStruct((rows, width), jnp.bfloat16),
        in_specs=[hbm] * 4,
        out_specs=hbm,
        scratch_shapes=[
            pltpu.SMEM(owners.shape, jnp.int32),
            pltpu.SMEM(ab_width.shape, jnp.int32),
            pltpu.VMEM((rows, blocks * tile), jnp.bfloat16),
            pltpu.VMEM((held, tile, width), jnp.bfloat16),
            pltpu.VMEM((rows, width), jnp.bfloat16),
            pltpu.SemaphoreType.DMA((2,)),
            pltpu.SemaphoreType.DMA((held,)),
            pltpu.SemaphoreType.DMA((2,)),
            pltpu.SemaphoreType.DMA((2,)),
        ],
        compiler_params=pltpu.CompilerParams(vmem_limit_bytes=limit),
    )(owners, ab_width, amps, panels)


def solution(mesh):
    placed = (
        P("grp", "blk"),
        P("grp", "blk"),
        P("blk"),
        P("grp", None, "blk"),
        P("grp", "blk"),
        P("blk"),
        P(),
    )
    return jax.shard_map(
        per_device, mesh=mesh, in_specs=placed, out_specs=P("grp", "blk"), check_vma=False
    )
```

```python
import functools

import jax
import jax.numpy as jnp
from jax import lax
from jax.experimental import pallas as pl
from jax.experimental.pallas import tpu as pltpu
from jax.sharding import PartitionSpec as P

UP, DOWN, PAIR, CROSSED = 0, 1, 2, 3


class Gather:
    def __init__(self, axis, count, split, own, slot_of, send_sem, recv_sem):
        me = lax.axis_index(axis)
        self.half, self.split = count // 2, split
        self.pos, self.side = me // 2, me % 2
        self.own, self.slot_of = own, slot_of
        self.send_sem, self.recv_sem = send_sem, recv_sem
        self.not_last = self.pos + 1 < self.half
        self.not_first = self.pos > 0
        self.up = {axis: jnp.minimum(self.pos + 1, self.half - 1) * 2 + self.side}
        self.down = {axis: jnp.maximum(self.pos - 1, 0) * 2 + self.side}
        self.pair = {axis: self.pos * 2 + 1 - self.side}

    def signal_all(self, barrier):
        def to(device):
            pl.semaphore_signal(
                barrier, inc=1, device_id=device, device_id_type=pl.DeviceIdType.MESH
            )

        to(self.pair)
        pl.when(self.not_last)(lambda: to(self.up))
        pl.when(self.not_first)(lambda: to(self.down))

    def neighbours(self):
        return 1 + self.not_last.astype(jnp.int32) + self.not_first.astype(jnp.int32)

    def copy(self, kind, h, p, own=False, other=False):
        slot = self.slot_of(p * 2 + (1 - self.side if other else self.side), h)
        row = kind * 2 + h if kind < CROSSED else 2 * CROSSED + h
        target = (self.up, self.down, self.pair, (self.up, self.down)[h])[kind]
        if kind == CROSSED:
            slot = self.slot_of(p * 2 + 1 - self.side, 0)
        return pltpu.make_async_remote_copy(
            src_ref=self.own(h) if own else slot,
            dst_ref=slot,
            send_sem=self.send_sem.at[row, p],
            recv_sem=self.recv_sem.at[row, p],
            device_id=target,
            device_id_type=pl.DeviceIdType.MESH,
        )

    def cross(self, p):
        return self.split & ((p == 0) | (p == self.half - 1))

    def begin(self):
        for h in (0, 1):
            self.copy(PAIR, h, self.pos, own=True).start()
        for h in (1, 0):
            pl.when(self.not_last)(lambda h=h: self.copy(UP, h, self.pos, own=True).start())
            pl.when(self.not_first)(lambda h=h: self.copy(DOWN, h, self.pos, own=True).start())

    def begin_crossed(self):
        for way, end, last in ((UP, 0, self.half - 1), (DOWN, self.half - 1, 0)):

            @pl.when(self.pos == end)
            def _(way=way, end=end):
                self.copy(PAIR, 0, end, other=True).wait_recv()
                self.copy(CROSSED, way, end).start()

    def steps(self, first, last):
        def arrived(way, h, p, going_on):
            self.copy(way, h, p).wait_recv()
            pl.when(going_on)(lambda: self.copy(way, h, p).start())
            if h == 1 or not self.split:
                self.copy(PAIR, h, p).start()
            else:
                pl.when(jnp.logical_not(self.cross(p)))(lambda: self.copy(PAIR, h, p).start())

        def crossed(way, p, going_on):
            self.copy(CROSSED, way, p).wait_recv()
            pl.when(going_on)(lambda: self.copy(CROSSED, way, p).start())

        def step(s, carry):
            below, above = self.pos - 1 - s, self.pos + 1 + s
            for h in (1, 0):
                pl.when(below >= 0)(lambda h=h: arrived(UP, h, below, self.not_last))
                pl.when(above < self.half)(lambda h=h: arrived(DOWN, h, above, self.not_first))
            if self.split:
                end = self.half - 1
                pl.when(below == 0)(lambda: crossed(UP, 0, self.not_last))
                pl.when(above == end)(lambda: crossed(DOWN, end, self.not_first))
            return carry

        lax.fori_loop(first, last, step, 0)

    def finish(self):
        def one(p, carry):
            self.copy(PAIR, 1, p, other=True).wait_recv()
            self.copy(PAIR, 1, p).wait_send()
            if self.split:

                @pl.when(jnp.logical_not(self.cross(p)))
                def _():
                    self.copy(PAIR, 0, p, other=True).wait_recv()
                    self.copy(PAIR, 0, p).wait_send()

                @pl.when(self.cross(p) & (p == self.pos))
                def _():
                    self.copy(PAIR, 0, p).wait_send()

            else:
                self.copy(PAIR, 0, p, other=True).wait_recv()
                self.copy(PAIR, 0, p).wait_send()

            @pl.when(self.not_last & (p <= self.pos))
            def _():
                for h in (0, 1):
                    self.copy(UP, h, p).wait_send()

            @pl.when(self.not_first & (p >= self.pos))
            def _():
                for h in (0, 1):
                    self.copy(DOWN, h, p).wait_send()

            return carry

        lax.fori_loop(0, self.half, one, 0)
        if self.split:
            pl.when(self.not_last)(lambda: self.copy(CROSSED, UP, 0).wait_send())
            pl.when(self.not_first)(lambda: self.copy(CROSSED, DOWN, self.half - 1).wait_send())


def gather_kernel(
    groups, blocks, amps, amp_tiles, cd_width, ints, int_tiles, panels, all_amps,
    own_panel, own_amps, amp_tiles_s, cd_width_s, int_tiles_s,
    panel_send, panel_recv, amp_send, amp_recv, local,
):
    rows, tile = own_amps.shape
    width = own_panel.shape[1]
    fetches = [
        pltpu.make_async_copy(source, target, local.at[i])
        for i, (source, target) in enumerate(
            (
                (int_tiles, int_tiles_s),
                (ints.at[0], own_panel),
                (amp_tiles, amp_tiles_s),
                (cd_width, cd_width_s),
                (amps, own_amps),
            )
        )
    ]
    for fetch in fetches:
        fetch.start()
    panel_gather = Gather(
        "grp", groups, True,
        lambda h: own_panel.at[pl.ds(h * (tile // 2), tile // 2)],
        lambda i, h: panels.at[i, pl.ds(h * (tile // 2), tile // 2)],
        panel_send, panel_recv,
    )
    amp_gather = Gather(
        "blk", blocks, False,
        lambda h: own_amps.at[pl.ds(h * (rows // 2), rows // 2)],
        lambda i, h: all_amps.at[
            pl.ds(h * (rows // 2), rows // 2), pl.ds(pl.multiple_of(i * tile, tile), tile)
        ],
        amp_send, amp_recv,
    )
    barrier = pltpu.get_barrier_semaphore()
    panel_gather.signal_all(barrier)
    amp_gather.signal_all(barrier)

    fetches[0].wait()
    fetches[1].wait()
    for j in range(width // tile):
        cols = slice(j * tile, (j + 1) * tile)
        keep = jnp.full((tile, tile), int_tiles_s[0, j], jnp.int32) > 0
        own_panel[:, cols] = jnp.where(
            keep, own_panel[:, cols].astype(jnp.float32), 0.0
        ).astype(jnp.bfloat16)
    pl.semaphore_wait(barrier, panel_gather.neighbours() + amp_gather.neighbours())
    panel_gather.begin()
    for fetch in fetches[2:]:
        fetch.wait()
    within = lax.broadcasted_iota(jnp.int32, (tile, tile), 1) < cd_width_s[0]
    for r in range(rows // tile):
        part = slice(r * tile, (r + 1) * tile)
        keep = (jnp.full((tile, tile), amp_tiles_s[0, r], jnp.int32) > 0) & within
        own_amps[part, :] = jnp.where(keep, own_amps[part, :].astype(jnp.float32), 0.0).astype(
            jnp.bfloat16
        )
    amp_gather.begin()
    mine = pl.ds(pl.multiple_of(lax.axis_index("blk") * tile, tile), tile)
    keeps = [
        pltpu.make_async_copy(own_panel, panels.at[lax.axis_index("grp")], local.at[0]),
        pltpu.make_async_copy(own_amps, all_amps.at[:, mine], local.at[1]),
    ]
    for keep in keeps:
        keep.start()
    panel_gather.begin_crossed()
    panel_gather.steps(0, 1)
    amp_gather.steps(0, blocks // 2 - 1)
    panel_gather.steps(1, groups // 2 - 1)
    for keep in keeps:
        keep.wait()
    amp_gather.finish()
    panel_gather.finish()


def multiply_kernel(
    owners, ab_width, amps, panels, out,
    owners_s, ab_width_s, all_amps, held, result, sem, held_sem, amp_sem, out_sem,
):
    tile = panels.shape[1]
    rows, width = out.shape
    count = owners.shape[0]
    part = rows // amp_sem.shape[0]
    whole = held.shape[0] == panels.shape[0]

    def rows_of(r):
        return pl.ds(pl.multiple_of(r * part, part), part)

    def fetch_amps(r):
        return pltpu.make_async_copy(
            amps.at[rows_of(r)], all_amps.at[rows_of(r)], amp_sem.at[r]
        )

    def store(r):
        return pltpu.make_async_copy(result.at[rows_of(r)], out.at[rows_of(r)], out_sem.at[r])

    scalars = [
        pltpu.make_async_copy(owners, owners_s, sem.at[0]),
        pltpu.make_async_copy(ab_width, ab_width_s, sem.at[1]),
    ]
    for fetch in scalars:
        fetch.start()
    if not whole:
        scalars[0].wait()
    fetches = [
        pltpu.make_async_copy(panels.at[i if whole else owners_s[i]], held.at[i], held_sem.at[i])
        for i in range(held.shape[0])
    ]
    for fetch in fetches:
        fetch.start()
    for r in range(rows // part):
        fetch_amps(r).start()
    if whole:
        scalars[0].wait()
    scalars[1].wait()
    for fetch in fetches:
        fetch.wait()
    column = lax.broadcasted_iota(jnp.int32, (1, 2 * tile), 1)

    def multiply(r, carry):
        fetch_amps(r).wait()
        for j in range(0, width // tile, 2):
            cols = slice(j * tile, (j + 2) * tile)
            chosen = jnp.concatenate(
                [held[owners_s[t] if whole else t, :, cols] for t in range(count)], axis=0
            )
            total = jnp.dot(
                all_amps[rows_of(r), :], chosen, preferred_element_type=jnp.float32
            )
            limit = jnp.where(column < tile, ab_width_s[j], tile + ab_width_s[j + 1])
            result[rows_of(r), cols] = jnp.where(column < limit, 0.5 * total, 0.0).astype(
                out.dtype
            )
        store(r).start()
        return carry

    parts = rows // part
    lax.fori_loop(0, parts, multiply, 0)
    lax.fori_loop(0, parts, lambda r, carry: (store(r).wait(), carry)[1], 0)


def per_device(amplitudes, amp_tiles, cd_width, integrals, int_tiles, ab_width, owners):
    rows, tile = amplitudes.shape
    width = integrals.shape[2]
    groups, blocks = lax.axis_size("grp"), lax.axis_size("blk")
    hbm = pl.BlockSpec(memory_space=pltpu.HBM)
    amp_tiles = amp_tiles.T
    limit = 60 * 2**20
    panels, amps = pl.pallas_call(
        functools.partial(gather_kernel, groups, blocks),
        out_shape=(
            jax.ShapeDtypeStruct((groups, tile, width), jnp.bfloat16),
            jax.ShapeDtypeStruct((rows, blocks * tile), jnp.bfloat16),
        ),
        in_specs=[hbm] * 5,
        out_specs=(hbm, hbm),
        scratch_shapes=[
            pltpu.VMEM((tile, width), jnp.bfloat16),
            pltpu.VMEM((rows, tile), jnp.bfloat16),
            pltpu.SMEM(amp_tiles.shape, jnp.int32),
            pltpu.SMEM(cd_width.shape, jnp.int32),
            pltpu.SMEM(int_tiles.shape, jnp.int32),
            pltpu.SemaphoreType.DMA((8, groups // 2)),
            pltpu.SemaphoreType.DMA((8, groups // 2)),
            pltpu.SemaphoreType.DMA((8, blocks // 2)),
            pltpu.SemaphoreType.DMA((8, blocks // 2)),
            pltpu.SemaphoreType.DMA((5,)),
        ],
        compiler_params=pltpu.CompilerParams(
            collective_id=0, has_side_effects=True, vmem_limit_bytes=limit
        ),
    )(amplitudes, amp_tiles, cd_width, integrals, int_tiles)
    held = groups if groups <= 2 * blocks else blocks
    return pl.pallas_call(
        multiply_kernel,
        out_shape=jax.ShapeDtypeStruct((rows, width), jnp.bfloat16),
        in_specs=[hbm] * 4,
        out_specs=hbm,
        scratch_shapes=[
            pltpu.SMEM(owners.shape, jnp.int32),
            pltpu.SMEM(ab_width.shape, jnp.int32),
            pltpu.VMEM((rows, blocks * tile), jnp.bfloat16),
            pltpu.VMEM((held, tile, width), jnp.bfloat16),
            pltpu.VMEM((rows, width), jnp.bfloat16),
            pltpu.SemaphoreType.DMA((2,)),
            pltpu.SemaphoreType.DMA((held,)),
            pltpu.SemaphoreType.DMA((2,)),
            pltpu.SemaphoreType.DMA((2,)),
        ],
        compiler_params=pltpu.CompilerParams(vmem_limit_bytes=limit),
    )(owners, ab_width, amps, panels)


def solution(mesh):
    placed = (
        P("grp", "blk"),
        P("grp", "blk"),
        P("blk"),
        P("grp", None, "blk"),
        P("grp", "blk"),
        P("blk"),
        P(),
    )
    return jax.shard_map(
        per_device, mesh=mesh, in_specs=placed, out_specs=P("grp", "blk"), check_vma=False
    )
```

```python
import functools

import jax
import jax.numpy as jnp
from jax import lax
from jax.experimental import pallas as pl
from jax.experimental.pallas import tpu as pltpu
from jax.sharding import PartitionSpec as P

UP, DOWN, PAIR, CROSSED = 0, 1, 2, 3


class Gather:
    def __init__(self, axis, count, split, own, slot_of, send_sem, recv_sem):
        me = lax.axis_index(axis)
        self.half, self.split = count // 2, split
        self.pos, self.side = me // 2, me % 2
        self.own, self.slot_of = own, slot_of
        self.send_sem, self.recv_sem = send_sem, recv_sem
        self.not_last = self.pos + 1 < self.half
        self.not_first = self.pos > 0
        self.up = {axis: jnp.minimum(self.pos + 1, self.half - 1) * 2 + self.side}
        self.down = {axis: jnp.maximum(self.pos - 1, 0) * 2 + self.side}
        self.pair = {axis: self.pos * 2 + 1 - self.side}

    def signal_all(self, barrier):
        def to(device):
            pl.semaphore_signal(
                barrier, inc=1, device_id=device, device_id_type=pl.DeviceIdType.MESH
            )

        to(self.pair)
        pl.when(self.not_last)(lambda: to(self.up))
        pl.when(self.not_first)(lambda: to(self.down))

    def neighbours(self):
        return 1 + self.not_last.astype(jnp.int32) + self.not_first.astype(jnp.int32)

    def copy(self, kind, h, p, own=False, other=False):
        slot = self.slot_of(p * 2 + (1 - self.side if other else self.side), h)
        row = kind * 2 + h if kind < CROSSED else 2 * CROSSED + h
        target = (self.up, self.down, self.pair, (self.up, self.down)[h])[kind]
        if kind == CROSSED:
            slot = self.slot_of(p * 2 + 1 - self.side, 0)
        return pltpu.make_async_remote_copy(
            src_ref=self.own(h) if own else slot,
            dst_ref=slot,
            send_sem=self.send_sem.at[row, p],
            recv_sem=self.recv_sem.at[row, p],
            device_id=target,
            device_id_type=pl.DeviceIdType.MESH,
        )

    def cross(self, p):
        return self.split & ((p == 0) | (p == self.half - 1))

    def begin(self):
        for h in (0, 1):
            self.copy(PAIR, h, self.pos, own=True).start()
        for h in (1, 0):
            pl.when(self.not_last)(lambda h=h: self.copy(UP, h, self.pos, own=True).start())
            pl.when(self.not_first)(lambda h=h: self.copy(DOWN, h, self.pos, own=True).start())

    def begin_crossed(self):
        for way, end, last in ((UP, 0, self.half - 1), (DOWN, self.half - 1, 0)):

            @pl.when(self.pos == end)
            def _(way=way, end=end):
                self.copy(PAIR, 0, end, other=True).wait_recv()
                self.copy(CROSSED, way, end).start()

    def steps(self, first, last):
        def arrived(way, h, p, going_on):
            self.copy(way, h, p).wait_recv()
            pl.when(going_on)(lambda: self.copy(way, h, p).start())
            if h == 1 or not self.split:
                self.copy(PAIR, h, p).start()
            else:
                pl.when(jnp.logical_not(self.cross(p)))(lambda: self.copy(PAIR, h, p).start())

        def crossed(way, p, going_on):
            self.copy(CROSSED, way, p).wait_recv()
            pl.when(going_on)(lambda: self.copy(CROSSED, way, p).start())

        def step(s, carry):
            below, above = self.pos - 1 - s, self.pos + 1 + s
            for h in (1, 0):
                pl.when(below >= 0)(lambda h=h: arrived(UP, h, below, self.not_last))
                pl.when(above < self.half)(lambda h=h: arrived(DOWN, h, above, self.not_first))
            if self.split:
                end = self.half - 1
                pl.when(below == 0)(lambda: crossed(UP, 0, self.not_last))
                pl.when(above == end)(lambda: crossed(DOWN, end, self.not_first))
            return carry

        lax.fori_loop(first, last, step, 0)

    def finish(self):
        def one(p, carry):
            self.copy(PAIR, 1, p, other=True).wait_recv()
            self.copy(PAIR, 1, p).wait_send()
            if self.split:

                @pl.when(jnp.logical_not(self.cross(p)))
                def _():
                    self.copy(PAIR, 0, p, other=True).wait_recv()
                    self.copy(PAIR, 0, p).wait_send()

                @pl.when(self.cross(p) & (p == self.pos))
                def _():
                    self.copy(PAIR, 0, p).wait_send()

            else:
                self.copy(PAIR, 0, p, other=True).wait_recv()
                self.copy(PAIR, 0, p).wait_send()

            @pl.when(self.not_last & (p <= self.pos))
            def _():
                for h in (0, 1):
                    self.copy(UP, h, p).wait_send()

            @pl.when(self.not_first & (p >= self.pos))
            def _():
                for h in (0, 1):
                    self.copy(DOWN, h, p).wait_send()

            return carry

        lax.fori_loop(0, self.half, one, 0)
        if self.split:
            pl.when(self.not_last)(lambda: self.copy(CROSSED, UP, 0).wait_send())
            pl.when(self.not_first)(lambda: self.copy(CROSSED, DOWN, self.half - 1).wait_send())


def gather_kernel(
    groups, blocks, amps, amp_tiles, cd_width, ints, int_tiles, panels, all_amps,
    own_panel, own_amps, amp_tiles_s, cd_width_s, int_tiles_s,
    panel_send, panel_recv, amp_send, amp_recv, local,
):
    rows, tile = own_amps.shape
    width = own_panel.shape[1]
    fetches = [
        pltpu.make_async_copy(source, target, local.at[i])
        for i, (source, target) in enumerate(
            (
                (int_tiles, int_tiles_s),
                (ints.at[0], own_panel),
                (amp_tiles, amp_tiles_s),
                (cd_width, cd_width_s),
                (amps, own_amps),
            )
        )
    ]
    for fetch in fetches:
        fetch.start()
    panel_gather = Gather(
        "grp", groups, True,
        lambda h: own_panel.at[pl.ds(h * (tile // 2), tile // 2)],
        lambda i, h: panels.at[i, pl.ds(h * (tile // 2), tile // 2)],
        panel_send, panel_recv,
    )
    amp_gather = Gather(
        "blk", blocks, False,
        lambda h: own_amps.at[pl.ds(h * (rows // 2), rows // 2)],
        lambda i, h: all_amps.at[
            pl.ds(h * (rows // 2), rows // 2), pl.ds(pl.multiple_of(i * tile, tile), tile)
        ],
        amp_send, amp_recv,
    )
    barrier = pltpu.get_barrier_semaphore()
    panel_gather.signal_all(barrier)
    amp_gather.signal_all(barrier)

    fetches[0].wait()
    fetches[1].wait()
    for j in range(width // tile):
        cols = slice(j * tile, (j + 1) * tile)
        keep = jnp.full((tile, tile), int_tiles_s[0, j], jnp.int32) > 0
        own_panel[:, cols] = jnp.where(
            keep, own_panel[:, cols].astype(jnp.float32), 0.0
        ).astype(jnp.bfloat16)
    pl.semaphore_wait(barrier, panel_gather.neighbours() + amp_gather.neighbours())
    panel_gather.begin()
    for fetch in fetches[2:]:
        fetch.wait()
    within = lax.broadcasted_iota(jnp.int32, (tile, tile), 1) < cd_width_s[0]
    for r in range(rows // tile):
        part = slice(r * tile, (r + 1) * tile)
        keep = (jnp.full((tile, tile), amp_tiles_s[0, r], jnp.int32) > 0) & within
        own_amps[part, :] = jnp.where(keep, own_amps[part, :].astype(jnp.float32), 0.0).astype(
            jnp.bfloat16
        )
    amp_gather.begin()
    mine = pl.ds(pl.multiple_of(lax.axis_index("blk") * tile, tile), tile)
    keeps = [
        pltpu.make_async_copy(own_panel, panels.at[lax.axis_index("grp")], local.at[0]),
        pltpu.make_async_copy(own_amps, all_amps.at[:, mine], local.at[1]),
    ]
    for keep in keeps:
        keep.start()
    panel_gather.begin_crossed()
    panel_gather.steps(0, 1)
    amp_gather.steps(0, blocks // 2 - 1)
    panel_gather.steps(1, groups // 2 - 1)
    for keep in keeps:
        keep.wait()
    amp_gather.finish()
    panel_gather.finish()


def multiply_kernel(
    owners, ab_width, amps, panels, out,
    owners_s, ab_width_s, all_amps, held, result, sem, held_sem, amp_sem, out_sem,
):
    tile = panels.shape[1]
    rows, width = out.shape
    count = owners.shape[0]
    part = rows // amp_sem.shape[0]
    whole = held.shape[0] == panels.shape[0]

    def rows_of(r):
        return pl.ds(pl.multiple_of(r * part, part), part)

    def fetch_amps(r):
        return pltpu.make_async_copy(
            amps.at[rows_of(r)], all_amps.at[rows_of(r)], amp_sem.at[r]
        )

    scalars = [
        pltpu.make_async_copy(owners, owners_s, sem.at[0]),
        pltpu.make_async_copy(ab_width, ab_width_s, sem.at[1]),
    ]
    for fetch in scalars:
        fetch.start()
    if not whole:
        scalars[0].wait()
    parts = held_sem.shape[0]
    span = width // parts

    def fetch_panel(c, i):
        cols = pl.ds(c * span, span)
        return pltpu.make_async_copy(
            panels.at[i if whole else owners_s[i], :, cols], held.at[i, :, cols], held_sem.at[c, i]
        )

    def store(c):
        cols = pl.ds(c * span, span)
        return pltpu.make_async_copy(result.at[:, cols], out.at[:, cols], out_sem.at[c])

    for r in range(rows // part):
        fetch_amps(r).start()
    for c in range(parts):
        for i in range(held.shape[0]):
            fetch_panel(c, i).start()
    if whole:
        scalars[0].wait()
    scalars[1].wait()
    for r in range(rows // part):
        fetch_amps(r).wait()
    column = lax.broadcasted_iota(jnp.int32, (1, 2 * tile), 1)
    for c in range(parts):
        for i in range(held.shape[0]):
            fetch_panel(c, i).wait()
        for j in range(c * span // tile, (c + 1) * span // tile, 2):
            cols = slice(j * tile, (j + 2) * tile)
            chosen = jnp.concatenate(
                [held[owners_s[t] if whole else t, :, cols] for t in range(count)], axis=0
            )
            total = jnp.dot(all_amps[...], chosen, preferred_element_type=jnp.float32)
            limit = jnp.where(column < tile, ab_width_s[j], tile + ab_width_s[j + 1])
            result[:, cols] = jnp.where(column < limit, 0.5 * total, 0.0).astype(out.dtype)
        store(c).start()
    for c in range(parts):
        store(c).wait()


def per_device(amplitudes, amp_tiles, cd_width, integrals, int_tiles, ab_width, owners):
    rows, tile = amplitudes.shape
    width = integrals.shape[2]
    groups, blocks = lax.axis_size("grp"), lax.axis_size("blk")
    hbm = pl.BlockSpec(memory_space=pltpu.HBM)
    amp_tiles = amp_tiles.T
    limit = 60 * 2**20
    panels, amps = pl.pallas_call(
        functools.partial(gather_kernel, groups, blocks),
        out_shape=(
            jax.ShapeDtypeStruct((groups, tile, width), jnp.bfloat16),
            jax.ShapeDtypeStruct((rows, blocks * tile), jnp.bfloat16),
        ),
        in_specs=[hbm] * 5,
        out_specs=(hbm, hbm),
        scratch_shapes=[
            pltpu.VMEM((tile, width), jnp.bfloat16),
            pltpu.VMEM((rows, tile), jnp.bfloat16),
            pltpu.SMEM(amp_tiles.shape, jnp.int32),
            pltpu.SMEM(cd_width.shape, jnp.int32),
            pltpu.SMEM(int_tiles.shape, jnp.int32),
            pltpu.SemaphoreType.DMA((8, groups // 2)),
            pltpu.SemaphoreType.DMA((8, groups // 2)),
            pltpu.SemaphoreType.DMA((8, blocks // 2)),
            pltpu.SemaphoreType.DMA((8, blocks // 2)),
            pltpu.SemaphoreType.DMA((5,)),
        ],
        compiler_params=pltpu.CompilerParams(
            collective_id=0, has_side_effects=True, vmem_limit_bytes=limit
        ),
    )(amplitudes, amp_tiles, cd_width, integrals, int_tiles)
    held = groups if groups <= 2 * blocks else blocks
    return pl.pallas_call(
        multiply_kernel,
        out_shape=jax.ShapeDtypeStruct((rows, width), jnp.bfloat16),
        in_specs=[hbm] * 4,
        out_specs=hbm,
        scratch_shapes=[
            pltpu.SMEM(owners.shape, jnp.int32),
            pltpu.SMEM(ab_width.shape, jnp.int32),
            pltpu.VMEM((rows, blocks * tile), jnp.bfloat16),
            pltpu.VMEM((held, tile, width), jnp.bfloat16),
            pltpu.VMEM((rows, width), jnp.bfloat16),
            pltpu.SemaphoreType.DMA((2,)),
            pltpu.SemaphoreType.DMA((2, held)),
            pltpu.SemaphoreType.DMA((2,)),
            pltpu.SemaphoreType.DMA((2,)),
        ],
        compiler_params=pltpu.CompilerParams(vmem_limit_bytes=limit),
    )(owners, ab_width, amps, panels)


def solution(mesh):
    placed = (
        P("grp", "blk"),
        P("grp", "blk"),
        P("blk"),
        P("grp", None, "blk"),
        P("grp", "blk"),
        P("blk"),
        P(),
    )
    return jax.shard_map(
        per_device, mesh=mesh, in_specs=placed, out_specs=P("grp", "blk"), check_vma=False
    )
```
